32 devices in a mesh: groups: 2 (over y), dp: 4 (over z), sub: 4 (over x, core).
Axes of the slice: x: 2, y: 2, z: 4, core: 2. Of those that a mesh axis runs over, the one named last changes fastest.
Arguments:
- activations: bfloat16 [8192, 14336], P(('groups', 'dp'), 'sub'), parts along dimension 0, may hold values from -6 to 6
- out_grads: bfloat16 [8192, 4096], P(('groups', 'dp'), 'sub'), parts along dimension 0, may hold values from -20 to 20
- proj_in: bfloat16 [14336, 32], P('sub'), may hold values from -0.046875 to 0.046875
- proj_out: bfloat16 [4096, 32], P('sub'), may hold values from -0.09375 to 0.09375
- lengths: int32 [256], P(('groups', 'dp', 'sub')), parts along dimension 0, may hold values from 1 to 32, 2048 in all
- query_grads: bfloat16 [256, 1024], P(('groups', 'dp', 'sub')), parts along dimension 0, may hold values from -6 to 6
Outputs:
- scores: float32 [256, 128], P(('groups', 'dp', 'sub')), parts along dimension 0
The draws below stay inside these ranges and needn't reach their ends.
There are 2 independent parts, one for each index of `groups`. The reference program is written for one: setup_inputs(seed, part) draws one part's arguments, and reference() takes and returns one part's arrays. A program takes and returns all parts, laid end to end along the dimension named above; an argument that names none is the same for every part. Nothing has to cross between parts.
Inputs may be any that keep to these rules, and one draw needn't show every extreme that they name: Within each group, the 128 lengths of that group sum to 2048, and one of them equals 32.
All inputs are finite; a program needn't handle non-finite values.
Results may differ from the reference program's by a relative error of at most 0.0003.
Values may be sent and summed in bfloat16 or wider, within the bound.
A program may use at most 128 MiB of HBM per device.

```python
import math
import jax
import jax.numpy as jnp
import numpy as np
from jax import lax

D = 4096
FF = 14336
R_IN = 32
R_OUT = 32
LEN = 32
K = 1024
EXAMPLES = 128
QUERIES = 128


def draw_out_grads(key, part):
    key = jax.random.fold_in(key, 7)
    base_key, scale_key = jax.random.split(key, 2)
    base = jnp.clip(jax.random.normal(base_key, (EXAMPLES, LEN, D), jnp.float32), -4.0, 4.0)
    spread = 1.15
    factor = jnp.exp(jax.random.uniform(scale_key, (EXAMPLES, 1, 1), jnp.float32, -spread, spread))
    return (base * factor).reshape(EXAMPLES * LEN, D).astype(jnp.bfloat16)


def steps_of(stream_key, dims, shards, smallest, top_value):
    gain, own = 1.0, jax.random.fold_in(stream_key, 6)
    for position, shards_of in shards:
        heights = jnp.exp(jax.random.uniform(jax.random.fold_in(own, position), (shards_of,), jnp.float32, smallest / len(shards), top_value / len(shards)))
        gain = gain * jnp.repeat(heights, dims[position] // shards_of).reshape([-1 if axis == position else 1 for axis in range(len(dims))])
    return gain


def split_up(amount, total, most, skew):
    portions = [(1 << 20) // math.isqrt(grade ** skew) + 1 for grade in range(2, amount + 1)]
    surplus, counts = total - most - (amount - 1), [1] * (amount - 1)
    while surplus > 0:
        movable = [i for i in range(amount - 1) if counts[i] < most]
        mass, budget = sum([portions[i] for i in movable]), surplus
        for i in movable:
            extra = min(most - counts[i], max(1, budget * portions[i] // mass), surplus)
            counts[i] = counts[i] + extra
            surplus = surplus - extra
    return np.array([most] + counts)


def uneven(own_key, amount, total, bound, lean):
    if amount == 2:
        one = jax.random.randint(own_key, (), max(1, total - bound), min(bound, total - 1) + 1)
        return jnp.stack([one, total - one])
    sizes = jnp.asarray(split_up(amount, total, bound, lean), jnp.int32)
    couples = (amount - 1) // 2
    donor, taker = sizes[1:1 + 2 * couples:2], sizes[2:2 + 2 * couples:2]
    margin = jnp.minimum(donor - 1, bound - taker)
    moved = jax.random.randint(jax.random.fold_in(own_key, 1), (couples,), 0, 1 << 20) % (margin + 1)
    sizes = sizes.at[1:1 + 2 * couples:2].set(donor - moved).at[2:2 + 2 * couples:2].set(taker + moved)
    return sizes[jax.random.permutation(jax.random.fold_in(own_key, 2), amount)]


def normal_values(rng, shape, scale, limit, pieces=(), held_as=jnp.bfloat16):
    entries = jax.random.normal(rng, shape, jnp.float32) * scale
    if len(pieces) > 0:
        entries = steps_of(rng, shape, pieces, -0.22, 0.18) * entries
    return jnp.clip(entries, min=-limit, max=limit).astype(held_as)


def setup_inputs(seed: int = 0, part: int = 0) -> dict:
    key_of = jax.random.split(jax.random.key(seed), 7)
    own_keys = jax.random.split(jax.random.fold_in(key_of[6], part), 7)
    return {
        "activations": normal_values(own_keys[0], (EXAMPLES * LEN, FF), 1.0, 6.0, ((0, 4), (1, 4))),
        "out_grads": draw_out_grads(jax.random.fold_in(jax.random.fold_in(key_of[6], part), 71), part),
        "proj_in": normal_values(key_of[2], (FF, R_IN), FF ** -0.5, 0.046875, ((0, 4),)),
        "proj_out": normal_values(key_of[3], (D, R_OUT), D ** -0.5, 0.09375, ((0, 4),)),
        "lengths": uneven(own_keys[4], EXAMPLES, EXAMPLES * LEN // 2, LEN, 1).astype(jnp.int32),
        "query_grads": normal_values(own_keys[5], (QUERIES, K), 1.0, 6.0, ((0, 16),)),
    }


def reference(activations, out_grads, proj_in, proj_out, lengths, query_grads):
    act_proj = jnp.dot(activations.astype(jnp.float32), proj_in.astype(jnp.float32), preferred_element_type=jnp.float32)
    grad_proj = jnp.dot(out_grads.astype(jnp.float32), proj_out.astype(jnp.float32), preferred_element_type=jnp.float32)
    num_ex = lengths.shape[0]
    positions = jnp.arange(LEN, dtype=jnp.int32)
    token_mask = (positions[None, :] < lengths[:, None]).astype(jnp.float32)
    grad_tok = grad_proj.reshape(num_ex, LEN, R_OUT) * token_mask[:, :, None]
    act_tok = act_proj.reshape(num_ex, LEN, R_IN)
    factors = jnp.einsum('eto,etn->eon', grad_tok, act_tok, precision=lax.Precision.HIGHEST)
    factors = factors.reshape(num_ex, R_OUT * R_IN)
    gram = jnp.dot(factors.T, factors, precision=lax.Precision.HIGHEST)
    width = R_OUT * R_IN
    mean_diag = jnp.trace(gram) / width
    system = gram / mean_diag + jnp.eye(width, dtype=jnp.float32)
    factor_low = jnp.linalg.cholesky(system)
    right_side = factors.T / jnp.sqrt(mean_diag)
    middle = lax.linalg.triangular_solve(factor_low, right_side, left_side=True, lower=True, transpose_a=False)
    solved = lax.linalg.triangular_solve(factor_low, middle, left_side=True, lower=True, transpose_a=True)
    queries = query_grads.astype(jnp.float32)
    return jnp.dot(solved.T, queries.T, precision=lax.Precision.HIGHEST)
```

```python
import functools

import jax
import jax.numpy as jnp
from jax import lax
from jax.experimental import pallas as pl
from jax.experimental.pallas import tpu as pltpu
from jax.sharding import PartitionSpec as P

LEN = 32
EX = 8
LANES = 128
STEPS = 7
HI = lax.Precision.HIGHEST
MESH = pl.DeviceIdType.MESH
NT = (((1,), (1,)), ((), ()))


def general(activations, out_grads, proj_in, proj_out, lengths, query_grads):
    local_ex = lengths.shape[0]
    width_in = proj_in.shape[1]
    width_out = proj_out.shape[1]
    width = width_in * width_out
    grad_part = jnp.dot(out_grads, proj_out, preferred_element_type=jnp.float32)
    act_part = jnp.dot(activations, proj_in, preferred_element_type=jnp.float32)
    projected = lax.psum_scatter(
        jnp.concatenate([grad_part, act_part], axis=1), "sub", scatter_dimension=0, tiled=True
    )
    positions = jnp.arange(LEN, dtype=jnp.int32)
    token_mask = (positions[None, :] < lengths[:, None]).astype(jnp.float32)
    grad_tok = projected[:, :width_out].reshape(local_ex, LEN, width_out) * token_mask[:, :, None]
    act_tok = projected[:, width_out:].reshape(local_ex, LEN, width_in)
    factors = jnp.einsum("eto,etn->eon", grad_tok, act_tok, precision=HI).reshape(local_ex, width)
    queries = lax.all_gather(query_grads, ("dp", "sub"), axis=0, tiled=True).astype(jnp.float32)
    right = lax.dot_general(factors, queries, NT, precision=HI)
    right = lax.all_gather(right, ("dp", "sub"), axis=0, tiled=True)
    every = lax.all_gather(factors, ("dp", "sub"), axis=0, tiled=True)
    gram = lax.dot_general(every, every, NT, precision=HI)
    mean_diag = jnp.trace(gram) / width
    system = gram / mean_diag + jnp.eye(gram.shape[0], dtype=jnp.float32)
    low = jnp.linalg.cholesky(system)
    middle = lax.linalg.triangular_solve(
        low, right / jnp.sqrt(mean_diag), left_side=True, lower=True, transpose_a=False
    )
    scores = lax.linalg.triangular_solve(low, middle, left_side=True, lower=True, transpose_a=True)
    place = lax.axis_index("dp") * lax.axis_size("sub") + lax.axis_index("sub")
    return lax.dynamic_slice_in_dim(scores, place * local_ex, local_ex, axis=0)


def kernel(
    act_hbm, grad_hbm, pin_hbm, pout_hbm, len_ref, q_ref, out_ref,
    act_v, grad_v, pin_v, pout_v, spread, part_out, part_in, fac,
    f_send, f_all, q_send, q_all, rs_send, rs_in, gb_send, gb_all,
    act_sem, grad_sem, w_sem, ps_sem, pr_sem, fs_sem, fr_sem, qs_sem, qr_sem,
    rss_sem, rsr_sem, gs_sem, gr_sem, inv_v,
):
    f32, bf16 = jnp.float32, jnp.bfloat16
    dp = lax.axis_index("dp")
    sub = lax.axis_index("sub")
    me = dp * 4 + sub
    core = lax.rem(sub, 2)
    chip = dp * 2 + sub // 2
    mate = sub + 1 - 2 * core
    cross = lax.rem(sub + 2, 4)
    cross_mate = lax.rem(mate + 2, 4)

    w_copies = [
        pltpu.make_async_copy(pout_hbm, pout_v, w_sem.at[0]),
        pltpu.make_async_copy(pin_hbm, pin_v, w_sem.at[1]),
    ]
    for c in w_copies:
        c.start()
    order = (cross_mate, cross, mate, sub)
    loads = []
    for i, b in enumerate(order):
        row = pl.multiple_of(b * 256, 256)
        group = [
            pltpu.make_async_copy(
                grad_hbm.at[pl.ds(row, 256)], grad_v.at[i], grad_sem.at[i]
            )
        ]
        for h in range(2):
            group.append(
                pltpu.make_async_copy(
                    act_hbm.at[pl.ds(pl.multiple_of(row + 128 * h, 128), 128)],
                    act_v.at[i, pl.ds(128 * h, 128)],
                    act_sem.at[i, h],
                )
            )
        for c in group:
            c.start()
        loads.append(group)

    peers = []
    for i in range(1, 16):
        p = lax.rem(me + i, 16)
        peers.append((p, {"dp": p // 4, "sub": lax.rem(p, 4)}))

    barrier = pltpu.get_barrier_semaphore()
    for _, where in peers:
        pl.semaphore_signal(barrier, inc=1, device_id=where, device_id_type=MESH)

    row = lax.broadcasted_iota(jnp.int32, (LANES, 1024), 0)
    col = lax.broadcasted_iota(jnp.int32, (LANES, 1024), 1)
    for h in range(2):
        spread[2 * h] = jnp.where(row == 64 * h + col // 32, 1.0, 0.0).astype(bf16)
        spread[2 * h + 1] = jnp.where(row == 64 * h + 32 + col % 32, 1.0, 0.0).astype(bf16)
    tok = lax.broadcasted_iota(jnp.int32, (LANES, LANES), 0)
    lane = lax.broadcasted_iota(jnp.int32, (LANES, LANES), 1)
    example = tok // LEN + jnp.where(lane >= 64, 4, 0)
    limit = jnp.zeros((LANES, LANES), jnp.int32)
    for e in range(EX):
        limit = jnp.where(example == e, len_ref[e], limit)
    live = (tok % LEN) < limit
    eye = jnp.where(tok == lane, 1.0, 0.0).astype(f32)

    q = q_ref[...].astype(f32)
    for s in range(8):
        q_send[s] = q[:, s * LANES:(s + 1) * LANES]
    pl.semaphore_wait(barrier, 15)

    def push(src, dst, ssem, rsem, where):
        c = pltpu.make_async_remote_copy(
            src_ref=src, dst_ref=dst, send_sem=ssem, recv_sem=rsem,
            device_id=where, device_id_type=MESH,
        )
        c.start()
        return c

    def arrive(dst, ssem, rsem, where):
        pltpu.make_async_remote_copy(
            src_ref=dst, dst_ref=dst, send_sem=ssem, recv_sem=rsem,
            device_id=where, device_id_type=MESH,
        ).wait_recv()

    sent = []
    for i, (p, where) in enumerate(peers):
        sent.append(push(q_send.at[p // 2], q_all.at[me], qs_sem.at[i], qr_sem.at[me], where))
    q_all[me] = q_send[chip]

    for c in w_copies:
        c.wait()

    def project(i):
        for c in loads[i]:
            c.wait()
        g = jnp.dot(grad_v[i], pout_v[...], preferred_element_type=f32)
        a = jnp.dot(act_v[i], pin_v[...], preferred_element_type=f32)
        return jnp.concatenate([g[:128], a[:128], g[128:], a[128:]], axis=1)

    to_mate, to_cross = {"sub": mate}, {"sub": cross}
    part_out[0] = project(0)
    sent.append(push(part_out.at[0], part_in.at[0], ps_sem.at[0], pr_sem.at[0], to_mate))
    block = project(1)
    arrive(part_in.at[0], ps_sem.at[0], pr_sem.at[0], to_mate)
    part_out[1] = block + part_in[0]
    sent.append(push(part_out.at[1], part_in.at[1], ps_sem.at[1], pr_sem.at[1], to_cross))
    part_out[2] = project(2)
    sent.append(push(part_out.at[2], part_in.at[2], ps_sem.at[2], pr_sem.at[2], to_mate))
    block = project(3)
    arrive(part_in.at[2], ps_sem.at[2], pr_sem.at[2], to_mate)
    block = block + part_in[2]
    arrive(part_in.at[1], ps_sem.at[1], pr_sem.at[1], to_cross)
    total = jnp.where(live, block + part_in[1], 0.0)

    t1 = total.astype(bf16)
    rest = total - t1.astype(f32)
    t2 = rest.astype(bf16)
    t3 = (rest - t2.astype(f32)).astype(bf16)

    def widen(m):
        return (
            jnp.dot(t1, spread[m], preferred_element_type=f32)
            + jnp.dot(t2, spread[m], preferred_element_type=f32)
            + jnp.dot(t3, spread[m], preferred_element_type=f32)
        )

    for h in range(2):
        prod = widen(2 * h) * widen(2 * h + 1)
        for e in range(4):
            fac[4 * h + e:4 * h + e + 1, :] = jnp.sum(
                prod[LEN * e:LEN * (e + 1)], axis=0, keepdims=True
            )
    for s in range(8):
        f_send[s] = fac[:, s * LANES:(s + 1) * LANES]
    for i, (p, where) in enumerate(peers):
        sent.append(push(f_send.at[p // 2], f_all.at[me], fs_sem.at[i], fr_sem.at[me], where))
    f_all[me] = f_send[chip]
    for i, (p, where) in enumerate(peers):
        arrive(q_all.at[p], qs_sem.at[i], qr_sem.at[p], where)
    for i, (p, where) in enumerate(peers):
        arrive(f_all.at[p], fs_sem.at[i], fr_sem.at[p], where)

    rows = f_all[pl.ds(core * 8, 8)].reshape(64, LANES)
    gram_part = lax.dot_general(
        rows, f_all[...].reshape(LANES, LANES), NT, precision=HI, preferred_element_type=f32
    )
    right_part = lax.dot_general(
        rows, q_all[...].reshape(LANES, LANES), NT, precision=HI, preferred_element_type=f32
    )
    rs_send[:, :, :LANES] = gram_part.reshape(8, 8, LANES)
    rs_send[:, :, LANES:] = right_part.reshape(8, 8, LANES)
    mates = []
    for i in range(1, 8):
        s = lax.rem(chip + i, 8)
        mates.append((s, {"dp": s // 2, "sub": lax.rem(s, 2) * 2 + core}))
    for i, (s, where) in enumerate(mates):
        sent.append(push(rs_send.at[s], rs_in.at[chip], rss_sem.at[i], rsr_sem.at[chip], where))
    rs_in[chip] = rs_send[chip]
    for i, (s, where) in enumerate(mates):
        arrive(rs_in.at[s], rss_sem.at[i], rsr_sem.at[s], where)
    gb_send[...] = jnp.sum(rs_in[...], axis=0)
    place = core * 8 + chip
    for i, (p, where) in enumerate(peers):
        sent.append(push(gb_send, gb_all.at[place], gs_sem.at[i], gr_sem.at[place], where))
    gb_all[place] = gb_send[...]
    for i, (p, where) in enumerate(peers):
        slot = lax.rem(p, 2) * 8 + p // 2
        arrive(gb_all.at[slot], gs_sem.at[i], gr_sem.at[slot], where)

    both = gb_all[...].reshape(LANES, 2 * LANES)
    gram, right = both[:, :LANES], both[:, LANES:]

    def dot(x, y):
        return jnp.dot(x, y, precision=HI, preferred_element_type=f32)

    def whole(x, op):
        return op(op(x, axis=0, keepdims=True), axis=1, keepdims=True)

    mean_diag = whole(gram * eye, jnp.sum) / 1024.0
    scaled = gram / mean_diag
    system = scaled + eye
    frob = jnp.sqrt(whole(scaled * scaled, jnp.sum))
    rowsum = jnp.max(jnp.sum(jnp.abs(scaled), axis=0, keepdims=True), axis=1, keepdims=True)
    top = 1.0 + 1.0001 * jnp.minimum(frob, rowsum)
    r = (top - 1.0) / (top + 1.0)
    start = 2.0 / (1.0 + top)
    res = eye - start * system
    inv = start * eye
    for k in range(STEPS):
        s = 2.0 / (2.0 - r * r)
        if k == 0:
            step = start * res
            square = dot(res, res)
        elif k < STEPS - 1:
            out = dot(jnp.concatenate([inv, res], axis=0), res)
            step, square = out[:LANES], out[LANES:]
        else:
            step = dot(inv, res)
        inv = s * (inv + step)
        if k < STEPS - 1:
            res = s * square + (1.0 - s) * eye
        r = r * r / (2.0 - r * r)
    right = right / jnp.sqrt(mean_diag)
    first = dot(inv, right)
    miss = right - dot(system, first)
    inv_v[0] = inv
    inv_v[1] = first
    mine = pl.ds(pl.multiple_of(me * EX, EX), EX)
    out_ref[...] = inv_v[1, mine, :] + dot(inv_v[0, mine, :], miss)

    for c in sent:
        c.wait_send()


def fused(activations, out_grads, proj_in, proj_out, lengths, query_grads):
    f32, bf16 = jnp.float32, jnp.bfloat16
    d_in, d_out = activations.shape[1], out_grads.shape[1]
    dma = pltpu.SemaphoreType.DMA
    return pl.pallas_call(
        kernel,
        out_shape=jax.ShapeDtypeStruct((EX, LANES), f32),
        in_specs=[pl.BlockSpec(memory_space=pl.ANY)] * 4
        + [pl.BlockSpec(memory_space=pltpu.SMEM), pl.BlockSpec(memory_space=pltpu.VMEM)],
        out_specs=pl.BlockSpec(memory_space=pltpu.VMEM),
        scratch_shapes=[
            pltpu.VMEM((4, 256, d_in), bf16),
            pltpu.VMEM((4, 256, d_out), bf16),
            pltpu.VMEM(proj_in.shape, bf16),
            pltpu.VMEM(proj_out.shape, bf16),
            pltpu.VMEM((4, LANES, 1024), bf16),
            pltpu.VMEM((3, LANES, LANES), f32),
            pltpu.VMEM((3, LANES, LANES), f32),
            pltpu.VMEM((EX, 1024), f32),
            pltpu.VMEM((8, 8, LANES), f32),
            pltpu.VMEM((16, 8, LANES), f32),
            pltpu.VMEM((8, 8, LANES), f32),
            pltpu.VMEM((16, 8, LANES), f32),
            pltpu.VMEM((8, 8, 2 * LANES), f32),
            pltpu.VMEM((8, 8, 2 * LANES), f32),
            pltpu.VMEM((8, 2 * LANES), f32),
            pltpu.VMEM((16, 8, 2 * LANES), f32),
            dma((4, 2)), dma((4,)), dma((2,)),
            dma((3,)), dma((3,)),
            dma((15,)), dma((16,)),
            dma((15,)), dma((16,)),
            dma((7,)), dma((8,)),
            dma((15,)), dma((16,)),
            pltpu.VMEM((2, LANES, LANES), f32),
        ],
        compiler_params=pltpu.CompilerParams(
            collective_id=0, has_side_effects=True, vmem_limit_bytes=50 * 1024 * 1024
        ),
    )(activations, out_grads, proj_in, proj_out, lengths, query_grads)


def per_device(small, activations, out_grads, proj_in, proj_out, lengths, query_grads):
    fits = (
        small
        and activations.shape[0] == EX * 4 * LEN
        and proj_in.shape[1] == 32
        and proj_out.shape[1] == 32
        and lengths.shape[0] == EX
        and query_grads.shape == (EX, 1024)
    )
    body = fused if fits else general
    return body(activations, out_grads, proj_in, proj_out, lengths, query_grads)


def solution(mesh):
    small = mesh.shape["dp"] == 4 and mesh.shape["sub"] == 4
    in_specs = (
        P(("groups", "dp"), "sub"),
        P(("groups", "dp"), "sub"),
        P("sub", None),
        P("sub", None),
        P(("groups", "dp", "sub")),
        P(("groups", "dp", "sub"), None),
    )
    out_specs = P(("groups", "dp", "sub"), None)
    return jax.shard_map(
        functools.partial(per_device, small),
        mesh=mesh, in_specs=in_specs, out_specs=out_specs, check_vma=False,
    )
```

```python
import functools

import jax
import jax.numpy as jnp
from jax import lax
from jax.experimental import pallas as pl
from jax.experimental.pallas import tpu as pltpu
from jax.sharding import PartitionSpec as P

LEN = 32
EX = 8
LANES = 128
STEPS = 7
HI = lax.Precision.HIGHEST
MESH = pl.DeviceIdType.MESH
NT = (((1,), (1,)), ((), ()))


def general(activations, out_grads, proj_in, proj_out, lengths, query_grads):
    local_ex = lengths.shape[0]
    width_in = proj_in.shape[1]
    width_out = proj_out.shape[1]
    width = width_in * width_out
    grad_part = jnp.dot(out_grads, proj_out, preferred_element_type=jnp.float32)
    act_part = jnp.dot(activations, proj_in, preferred_element_type=jnp.float32)
    projected = lax.psum_scatter(
        jnp.concatenate([grad_part, act_part], axis=1), "sub", scatter_dimension=0, tiled=True
    )
    positions = jnp.arange(LEN, dtype=jnp.int32)
    token_mask = (positions[None, :] < lengths[:, None]).astype(jnp.float32)
    grad_tok = projected[:, :width_out].reshape(local_ex, LEN, width_out) * token_mask[:, :, None]
    act_tok = projected[:, width_out:].reshape(local_ex, LEN, width_in)
    factors = jnp.einsum("eto,etn->eon", grad_tok, act_tok, precision=HI).reshape(local_ex, width)
    queries = lax.all_gather(query_grads, ("dp", "sub"), axis=0, tiled=True).astype(jnp.float32)
    right = lax.dot_general(factors, queries, NT, precision=HI)
    right = lax.all_gather(right, ("dp", "sub"), axis=0, tiled=True)
    every = lax.all_gather(factors, ("dp", "sub"), axis=0, tiled=True)
    gram = lax.dot_general(every, every, NT, precision=HI)
    mean_diag = jnp.trace(gram) / width
    system = gram / mean_diag + jnp.eye(gram.shape[0], dtype=jnp.float32)
    low = jnp.linalg.cholesky(system)
    middle = lax.linalg.triangular_solve(
        low, right / jnp.sqrt(mean_diag), left_side=True, lower=True, transpose_a=False
    )
    scores = lax.linalg.triangular_solve(low, middle, left_side=True, lower=True, transpose_a=True)
    place = lax.axis_index("dp") * lax.axis_size("sub") + lax.axis_index("sub")
    return lax.dynamic_slice_in_dim(scores, place * local_ex, local_ex, axis=0)


def kernel(
    act_hbm, grad_hbm, pin_hbm, pout_hbm, len_hbm, q_hbm, out_ref,
    act_v, grad_v, pin_v, pout_v, len_v, q_v, spread, part_out, part_in, fac,
    f_all, q_all, q_full, inv_v,
    act_sem, grad_sem, w_sem, ps_sem, pr_sem, fs_sem, fr_sem, qs_sem, qr_sem,
):
    f32, bf16 = jnp.float32, jnp.bfloat16
    dp = lax.axis_index("dp")
    sub = lax.axis_index("sub")
    me = dp * 4 + sub
    core = lax.rem(sub, 2)
    chip = dp * 2 + sub // 2
    mate = sub + 1 - 2 * core
    cross = lax.rem(sub + 2, 4)
    cross_mate = lax.rem(mate + 2, 4)

    to_mate, to_cross = {"sub": mate}, {"sub": cross}
    peers = []
    for dz, dx in ((2, 1), (1, 1), (3, 1), (2, 0), (1, 0), (3, 0), (0, 1)):
        z, u = lax.rem(dp + dz, 4), lax.rem(sub + 2 * dx, 4)
        peers.append((z * 4 + u, {"dp": z, "sub": u}))
    barrier = pltpu.get_barrier_semaphore()
    for where in [w for _, w in peers] + [to_mate]:
        pl.semaphore_signal(barrier, inc=1, device_id=where, device_id_type=MESH)

    w_copies = [
        pltpu.make_async_copy(pout_hbm, pout_v, w_sem.at[0]),
        pltpu.make_async_copy(pin_hbm, pin_v, w_sem.at[1]),
        pltpu.make_async_copy(len_hbm, len_v, w_sem.at[2]),
        pltpu.make_async_copy(q_hbm, q_v, w_sem.at[3]),
    ]
    for c in w_copies:
        c.start()
    order = (cross_mate, cross, mate, sub)
    loads = []
    for i, b in enumerate(order):
        row = pl.multiple_of(b * 256, 256)
        group = [
            pltpu.make_async_copy(
                grad_hbm.at[pl.ds(row, 256)], grad_v.at[i], grad_sem.at[i]
            )
        ]
        for h in range(2):
            group.append(
                pltpu.make_async_copy(
                    act_hbm.at[pl.ds(pl.multiple_of(row + 128 * h, 128), 128)],
                    act_v.at[i, pl.ds(128 * h, 128)],
                    act_sem.at[i, h],
                )
            )
        for c in group:
            c.start()
        loads.append(group)

    row = lax.broadcasted_iota(jnp.int32, (64, 1024), 0)
    col = lax.broadcasted_iota(jnp.int32, (64, 1024), 1)
    spread[0] = jnp.where(row == col // 32, 1.0, 0.0).astype(bf16)
    spread[1] = jnp.where(row == 32 + col % 32, 1.0, 0.0).astype(bf16)
    tok = lax.broadcasted_iota(jnp.int32, (LANES, LANES), 0)
    lane = lax.broadcasted_iota(jnp.int32, (LANES, LANES), 1)
    eye = jnp.where(tok == lane, 1.0, 0.0).astype(f32)

    def push(src, dst, ssem, rsem, where):
        c = pltpu.make_async_remote_copy(
            src_ref=src, dst_ref=dst, send_sem=ssem, recv_sem=rsem,
            device_id=where, device_id_type=MESH,
        )
        c.start()
        return c

    def arrive(dst, ssem, rsem, where):
        pltpu.make_async_remote_copy(
            src_ref=dst, dst_ref=dst, send_sem=ssem, recv_sem=rsem,
            device_id=where, device_id_type=MESH,
        ).wait_recv()

    sent = []
    for c in w_copies:
        c.wait()
    q = q_v[...].astype(f32)
    q_all[me] = jnp.concatenate([q[:, :512], q[:, 512:]], axis=0).astype(bf16)
    token = lax.broadcasted_iota(jnp.int32, (8, 256), 1)
    limit = jnp.zeros((8, 256), jnp.int32)
    for e in range(EX):
        limit = jnp.where(token // LEN == e, len_v[e], limit)
    live = jnp.where(token % LEN < limit, 1.0, 0.0)[:1]

    def project(i):
        for c in loads[i]:
            c.wait()
        g = lax.dot_general(pout_v[...], grad_v[i], NT, preferred_element_type=f32)
        a = lax.dot_general(pin_v[...], act_v[i], NT, preferred_element_type=f32)
        return jnp.concatenate([g, a], axis=0)

    part_out[0] = project(0)
    pl.semaphore_wait(barrier, 8)
    sent.append(push(part_out.at[0], part_in.at[0], ps_sem.at[0], pr_sem.at[0], to_mate))
    block = project(1)
    arrive(part_in.at[0], ps_sem.at[0], pr_sem.at[0], to_mate)
    part_out[1] = block + part_in[0]
    sent.append(push(part_out.at[1], part_in.at[1], ps_sem.at[1], pr_sem.at[1], to_cross))
    hosts = peers + [(me + mate - sub, to_mate)]
    for i, (p, where) in enumerate(hosts):
        sent.append(push(q_all.at[me], q_all.at[me], qs_sem.at[i], qr_sem.at[me], where))
    part_out[2] = project(2)
    sent.append(push(part_out.at[2], part_in.at[2], ps_sem.at[2], pr_sem.at[2], to_mate))
    block = project(3)
    arrive(part_in.at[2], ps_sem.at[2], pr_sem.at[2], to_mate)
    block = block + part_in[2]
    arrive(part_in.at[1], ps_sem.at[1], pr_sem.at[1], to_cross)
    total = ((block + part_in[1]) * live).T

    t1 = total.astype(bf16)
    rest = total - t1.astype(f32)
    t2 = rest.astype(bf16)
    t3 = (rest - t2.astype(f32)).astype(bf16)

    def widen(m):
        return (
            jnp.dot(t1, spread[m], preferred_element_type=f32)
            + jnp.dot(t2, spread[m], preferred_element_type=f32)
            + jnp.dot(t3, spread[m], preferred_element_type=f32)
        )

    prod = widen(0) * widen(1)
    for e in range(EX):
        fac[e:e + 1, :] = jnp.sum(prod[LEN * e:LEN * (e + 1)], axis=0, keepdims=True)
    f_all[me] = fac[...]
    for i, (p, where) in enumerate(hosts):
        sent.append(push(fac, f_all.at[me], fs_sem.at[i], fr_sem.at[me], where))
    for i, (p, where) in enumerate(peers):
        arrive(q_all.at[p], qs_sem.at[i], qr_sem.at[p], where)
        sent.append(push(q_all.at[p], q_all.at[p], qs_sem.at[8 + i], qr_sem.at[p], to_mate))
    for i, (p, where) in enumerate(hosts):
        slot = p + mate - sub if i < 7 else p
        arrive(q_all.at[slot], qs_sem.at[i], qr_sem.at[slot], to_mate)
    for d in range(16):
        q = q_all[d].astype(f32)
        q_full[8 * d:8 * d + 8, :512] = q[:8]
        q_full[8 * d:8 * d + 8, 512:] = q[8:]
    for i in (6, 4, 5, 3, 1, 2, 0):
        p, where = peers[i]
        arrive(f_all.at[p], fs_sem.at[i], fr_sem.at[p], where)
        sent.append(push(f_all.at[p], f_all.at[p], fs_sem.at[8 + i], fr_sem.at[p], to_mate))
    for i, (p, where) in enumerate(hosts):
        slot = p + mate - sub if i < 7 else p
        arrive(f_all.at[slot], fs_sem.at[i], fr_sem.at[slot], to_mate)

    every = f_all[...].reshape(LANES, 1024)
    gram = lax.dot_general(every, every, NT, precision=HI, preferred_element_type=f32)
    right = lax.dot_general(
        every, q_full[...], NT, precision=HI, preferred_element_type=f32
    )

    def dot(x, y):
        return jnp.dot(x, y, precision=HI, preferred_element_type=f32)

    def whole(x, op):
        return op(op(x, axis=0, keepdims=True), axis=1, keepdims=True)

    mean_diag = whole(gram * eye, jnp.sum) / 1024.0
    scaled = gram / mean_diag
    system = scaled + eye
    frob = jnp.sqrt(whole(scaled * scaled, jnp.sum))
    rowsum = jnp.max(jnp.sum(jnp.abs(scaled), axis=0, keepdims=True), axis=1, keepdims=True)
    top = 1.0 + 1.0001 * jnp.minimum(frob, rowsum)
    r = (top - 1.0) / (top + 1.0)
    start = 2.0 / (1.0 + top)
    res = eye - start * system
    inv = start * eye
    for k in range(STEPS):
        s = 2.0 / (2.0 - r * r)
        if k == 0:
            step = start * res
            square = dot(res, res)
        elif k < STEPS - 1:
            out = dot(jnp.concatenate([inv, res], axis=0), res)
            step, square = out[:LANES], out[LANES:]
        else:
            step = dot(inv, res)
        inv = s * (inv + step)
        if k < STEPS - 1:
            res = s * square + (1.0 - s) * eye
        r = r * r / (2.0 - r * r)
    right = right / jnp.sqrt(mean_diag)
    first = dot(inv, right)
    miss = right - dot(system, first)
    inv_v[0] = inv
    inv_v[1] = first
    mine = pl.ds(pl.multiple_of(me * EX, EX), EX)
    out_ref[...] = inv_v[1, mine, :] + dot(inv_v[0, mine, :], miss)

    for c in sent:
        c.wait_send()


def fused(activations, out_grads, proj_in, proj_out, lengths, query_grads):
    f32, bf16 = jnp.float32, jnp.bfloat16
    d_in, d_out = activations.shape[1], out_grads.shape[1]
    dma = pltpu.SemaphoreType.DMA
    return pl.pallas_call(
        kernel,
        out_shape=jax.ShapeDtypeStruct((EX, LANES), f32),
        in_specs=[pl.BlockSpec(memory_space=pl.ANY)] * 6,
        out_specs=pl.BlockSpec(memory_space=pltpu.VMEM),
        scratch_shapes=[
            pltpu.VMEM((4, 256, d_in), bf16),
            pltpu.VMEM((4, 256, d_out), bf16),
            pltpu.VMEM(proj_in.shape[::-1], bf16),
            pltpu.VMEM(proj_out.shape[::-1], bf16),
            pltpu.SMEM(lengths.shape, jnp.int32),
            pltpu.VMEM(query_grads.shape, bf16),
            pltpu.VMEM((2, 64, 1024), bf16),
            pltpu.VMEM((3, 64, 256), f32),
            pltpu.VMEM((3, 64, 256), f32),
            pltpu.VMEM((EX, 1024), f32),
            pltpu.VMEM((16, EX, 1024), f32),
            pltpu.VMEM((16, 16, 512), bf16),
            pltpu.VMEM((LANES, 1024), f32),
            pltpu.VMEM((2, LANES, LANES), f32),
            dma((4, 2)), dma((4,)), dma((4,)),
            dma((3,)), dma((3,)),
            dma((15,)), dma((16,)),
            dma((15,)), dma((16,)),
        ],
        compiler_params=pltpu.CompilerParams(
            collective_id=0, has_side_effects=True, vmem_limit_bytes=63 * 1024 * 1024
        ),
    )(activations, out_grads, proj_in.T, proj_out.T, lengths, query_grads)


def per_device(small, activations, out_grads, proj_in, proj_out, lengths, query_grads):
    fits = (
        small
        and activations.shape[0] == EX * 4 * LEN
        and proj_in.shape[1] == 32
        and proj_out.shape[1] == 32
        and lengths.shape[0] == EX
        and query_grads.shape == (EX, 1024)
    )
    body = fused if fits else general
    return body(activations, out_grads, proj_in, proj_out, lengths, query_grads)


def solution(mesh):
    small = mesh.shape["dp"] == 4 and mesh.shape["sub"] == 4
    in_specs = (
        P(("groups", "dp"), "sub"),
        P(("groups", "dp"), "sub"),
        P("sub", None),
        P("sub", None),
        P(("groups", "dp", "sub")),
        P(("groups", "dp", "sub"), None),
    )
    out_specs = P(("groups", "dp", "sub"), None)
    return jax.shard_map(
        functools.partial(per_device, small),
        mesh=mesh, in_specs=in_specs, out_specs=out_specs, check_vma=False,
    )
```

```python
import functools

import jax
import jax.numpy as jnp
from jax import lax
from jax.experimental import pallas as pl
from jax.experimental.pallas import tpu as pltpu
from jax.sharding import PartitionSpec as P

LEN = 32
EX = 8
LANES = 128
STEPS = 7
HI = lax.Precision.HIGHEST
MESH = pl.DeviceIdType.MESH
NT = (((1,), (1,)), ((), ()))


def general(activations, out_grads, proj_in, proj_out, lengths, query_grads):
    local_ex = lengths.shape[0]
    width_in = proj_in.shape[1]
    width_out = proj_out.shape[1]
    width = width_in * width_out
    grad_part = jnp.dot(out_grads, proj_out, preferred_element_type=jnp.float32)
    act_part = jnp.dot(activations, proj_in, preferred_element_type=jnp.float32)
    projected = lax.psum_scatter(
        jnp.concatenate([grad_part, act_part], axis=1), "sub", scatter_dimension=0, tiled=True
    )
    positions = jnp.arange(LEN, dtype=jnp.int32)
    token_mask = (positions[None, :] < lengths[:, None]).astype(jnp.float32)
    grad_tok = projected[:, :width_out].reshape(local_ex, LEN, width_out) * token_mask[:, :, None]
    act_tok = projected[:, width_out:].reshape(local_ex, LEN, width_in)
    factors = jnp.einsum("eto,etn->eon", grad_tok, act_tok, precision=HI).reshape(local_ex, width)
    queries = lax.all_gather(query_grads, ("dp", "sub"), axis=0, tiled=True).astype(jnp.float32)
    right = lax.dot_general(factors, queries, NT, precision=HI)
    right = lax.all_gather(right, ("dp", "sub"), axis=0, tiled=True)
    every = lax.all_gather(factors, ("dp", "sub"), axis=0, tiled=True)
    gram = lax.dot_general(every, every, NT, precision=HI)
    mean_diag = jnp.trace(gram) / width
    system = gram / mean_diag + jnp.eye(gram.shape[0], dtype=jnp.float32)
    low = jnp.linalg.cholesky(system)
    middle = lax.linalg.triangular_solve(
        low, right / jnp.sqrt(mean_diag), left_side=True, lower=True, transpose_a=False
    )
    scores = lax.linalg.triangular_solve(low, middle, left_side=True, lower=True, transpose_a=True)
    place = lax.axis_index("dp") * lax.axis_size("sub") + lax.axis_index("sub")
    return lax.dynamic_slice_in_dim(scores, place * local_ex, local_ex, axis=0)


def kernel(
    act_hbm, grad_hbm, pin_hbm, pout_hbm, len_hbm, q_hbm, out_ref,
    act_v, grad_v, pin_v, pout_v, len_v, q_v, spread, part_out, part_in, fac,
    f_all, q_all, q_full, inv_v,
    act_sem, grad_sem, w_sem, ps_sem, pr_sem, fs_sem, fr_sem, qs_sem, qr_sem,
):
    f32, bf16 = jnp.float32, jnp.bfloat16
    dp = lax.axis_index("dp")
    sub = lax.axis_index("sub")
    me = dp * 4 + sub
    core = lax.rem(sub, 2)
    chip = dp * 2 + sub // 2
    mate = sub + 1 - 2 * core
    cross = lax.rem(sub + 2, 4)
    cross_mate = lax.rem(mate + 2, 4)

    to_mate, to_cross = {"sub": mate}, {"sub": cross}
    peers = []
    for dz, dx in ((2, 1), (1, 1), (3, 1), (2, 0), (1, 0), (3, 0), (0, 1)):
        z, u = lax.rem(dp + dz, 4), lax.rem(sub + 2 * dx, 4)
        peers.append((z * 4 + u, {"dp": z, "sub": u}))
    barrier = pltpu.get_barrier_semaphore()
    for where in [w for _, w in peers] + [to_mate]:
        pl.semaphore_signal(barrier, inc=1, device_id=where, device_id_type=MESH)

    w_copies = [
        pltpu.make_async_copy(pout_hbm, pout_v, w_sem.at[0]),
        pltpu.make_async_copy(pin_hbm, pin_v, w_sem.at[1]),
        pltpu.make_async_copy(len_hbm, len_v, w_sem.at[2]),
        pltpu.make_async_copy(q_hbm, q_v, w_sem.at[3]),
    ]
    for c in w_copies:
        c.start()
    order = (cross_mate, cross, mate, sub)
    loads = []
    for i, b in enumerate(order):
        row = pl.multiple_of(b * 256, 256)
        group = [
            pltpu.make_async_copy(
                grad_hbm.at[pl.ds(row, 256)], grad_v.at[i], grad_sem.at[i]
            )
        ]
        for h in range(2):
            group.append(
                pltpu.make_async_copy(
                    act_hbm.at[pl.ds(pl.multiple_of(row + 128 * h, 128), 128)],
                    act_v.at[i, pl.ds(128 * h, 128)],
                    act_sem.at[i, h],
                )
            )
        for c in group:
            c.start()
        loads.append(group)

    row = lax.broadcasted_iota(jnp.int32, (64, 1024), 0)
    col = lax.broadcasted_iota(jnp.int32, (64, 1024), 1)
    spread[0] = jnp.where(row == col // 32, 1.0, 0.0).astype(bf16)
    spread[1] = jnp.where(row == 32 + col % 32, 1.0, 0.0).astype(bf16)
    tok = lax.broadcasted_iota(jnp.int32, (LANES, LANES), 0)
    lane = lax.broadcasted_iota(jnp.int32, (LANES, LANES), 1)
    eye = jnp.where(tok == lane, 1.0, 0.0).astype(f32)

    def push(src, dst, ssem, rsem, where):
        c = pltpu.make_async_remote_copy(
            src_ref=src, dst_ref=dst, send_sem=ssem, recv_sem=rsem,
            device_id=where, device_id_type=MESH,
        )
        c.start()
        return c

    def arrive(dst, ssem, rsem, where):
        pltpu.make_async_remote_copy(
            src_ref=dst, dst_ref=dst, send_sem=ssem, recv_sem=rsem,
            device_id=where, device_id_type=MESH,
        ).wait_recv()

    sent = []
    for c in w_copies:
        c.wait()
    q = q_v[...].astype(f32)
    q_all[me] = jnp.concatenate([q[:, :512], q[:, 512:]], axis=0).astype(bf16)
    token = lax.broadcasted_iota(jnp.int32, (8, 256), 1)
    limit = jnp.zeros((8, 256), jnp.int32)
    for e in range(EX):
        limit = jnp.where(token // LEN == e, len_v[e], limit)
    live = jnp.where(token % LEN < limit, 1.0, 0.0)[:1]

    def project(i):
        for c in loads[i]:
            c.wait()
        g = lax.dot_general(pout_v[...], grad_v[i], NT, preferred_element_type=f32)
        a = lax.dot_general(pin_v[...], act_v[i], NT, preferred_element_type=f32)
        return jnp.concatenate([g, a], axis=0)

    pl.semaphore_wait(barrier, 8)
    hosts = peers + [(me + mate - sub, to_mate)]
    for i, (p, where) in enumerate(hosts):
        sent.append(push(q_all.at[me], q_all.at[me], qs_sem.at[i], qr_sem.at[me], where))
    part_out[0] = project(0)
    sent.append(push(part_out.at[0], part_in.at[0], ps_sem.at[0], pr_sem.at[0], to_mate))
    block = project(1)
    arrive(part_in.at[0], ps_sem.at[0], pr_sem.at[0], to_mate)
    part_out[1] = block + part_in[0]
    sent.append(push(part_out.at[1], part_in.at[1], ps_sem.at[1], pr_sem.at[1], to_cross))
    part_out[2] = project(2)
    sent.append(push(part_out.at[2], part_in.at[2], ps_sem.at[2], pr_sem.at[2], to_mate))
    block = project(3)
    arrive(part_in.at[2], ps_sem.at[2], pr_sem.at[2], to_mate)
    block = block + part_in[2]
    arrive(part_in.at[1], ps_sem.at[1], pr_sem.at[1], to_cross)
    total = ((block + part_in[1]) * live).T

    t1 = total.astype(bf16)
    rest = total - t1.astype(f32)
    t2 = rest.astype(bf16)
    t3 = (rest - t2.astype(f32)).astype(bf16)

    def widen(m):
        return (
            jnp.dot(t1, spread[m], preferred_element_type=f32)
            + jnp.dot(t2, spread[m], preferred_element_type=f32)
            + jnp.dot(t3, spread[m], preferred_element_type=f32)
        )

    prod = widen(0) * widen(1)
    for e in range(EX):
        fac[e:e + 1, :] = jnp.sum(prod[LEN * e:LEN * (e + 1)], axis=0, keepdims=True)
    f_all[me] = fac[...]
    for i, (p, where) in enumerate(hosts):
        sent.append(push(fac, f_all.at[me], fs_sem.at[i], fr_sem.at[me], where))
    for i, (p, where) in enumerate(peers):
        arrive(q_all.at[p], qs_sem.at[i], qr_sem.at[p], where)
        sent.append(push(q_all.at[p], q_all.at[p], qs_sem.at[8 + i], qr_sem.at[p], to_mate))
    for i, (p, where) in enumerate(hosts):
        slot = p + mate - sub if i < 7 else p
        arrive(q_all.at[slot], qs_sem.at[i], qr_sem.at[slot], to_mate)
    for d in range(16):
        q = q_all[d].astype(f32)
        q_full[8 * d:8 * d + 8, :512] = q[:8]
        q_full[8 * d:8 * d + 8, 512:] = q[8:]
    for i in (6, 4, 5, 3, 1, 2, 0):
        p, where = peers[i]
        arrive(f_all.at[p], fs_sem.at[i], fr_sem.at[p], where)
        sent.append(push(f_all.at[p], f_all.at[p], fs_sem.at[8 + i], fr_sem.at[p], to_mate))
    for i, (p, where) in enumerate(hosts):
        slot = p + mate - sub if i < 7 else p
        arrive(f_all.at[slot], fs_sem.at[i], fr_sem.at[slot], to_mate)

    every = f_all[...].reshape(LANES, 1024)
    gram = lax.dot_general(every, every, NT, precision=HI, preferred_element_type=f32)
    right = lax.dot_general(
        every, q_full[...], NT, precision=HI, preferred_element_type=f32
    )

    def dot(x, y):
        return jnp.dot(x, y, precision=HI, preferred_element_type=f32)

    def whole(x, op):
        return op(op(x, axis=0, keepdims=True), axis=1, keepdims=True)

    mean_diag = whole(gram * eye, jnp.sum) / 1024.0
    scaled = gram / mean_diag
    system = scaled + eye
    frob = jnp.sqrt(whole(scaled * scaled, jnp.sum))
    rowsum = jnp.max(jnp.sum(jnp.abs(scaled), axis=0, keepdims=True), axis=1, keepdims=True)
    top = 1.0 + 1.0001 * jnp.minimum(frob, rowsum)
    r = (top - 1.0) / (top + 1.0)
    start = 2.0 / (1.0 + top)
    res = eye - start * system
    inv = start * eye
    for k in range(STEPS):
        s = 2.0 / (2.0 - r * r)
        if k == 0:
            step = start * res
            square = dot(res, res)
        elif k < STEPS - 1:
            out = dot(jnp.concatenate([inv, res], axis=0), res)
            step, square = out[:LANES], out[LANES:]
        else:
            step = dot(inv, res)
        inv = s * (inv + step)
        if k < STEPS - 1:
            res = s * square + (1.0 - s) * eye
        r = r * r / (2.0 - r * r)
    right = right / jnp.sqrt(mean_diag)
    first = dot(inv, right)
    miss = right - dot(system, first)
    inv_v[0] = inv
    inv_v[1] = first
    mine = pl.ds(pl.multiple_of(me * EX, EX), EX)
    out_ref[...] = inv_v[1, mine, :] + dot(inv_v[0, mine, :], miss)

    for c in sent:
        c.wait_send()


def fused(activations, out_grads, proj_in, proj_out, lengths, query_grads):
    f32, bf16 = jnp.float32, jnp.bfloat16
    d_in, d_out = activations.shape[1], out_grads.shape[1]
    dma = pltpu.SemaphoreType.DMA
    return pl.pallas_call(
        kernel,
        out_shape=pltpu.VMEM((EX, LANES), f32),
        in_specs=[pl.BlockSpec(memory_space=pl.ANY)] * 6,
        out_specs=pl.BlockSpec(memory_space=pltpu.VMEM),
        scratch_shapes=[
            pltpu.VMEM((4, 256, d_in), bf16),
            pltpu.VMEM((4, 256, d_out), bf16),
            pltpu.VMEM(proj_in.shape[::-1], bf16),
            pltpu.VMEM(proj_out.shape[::-1], bf16),
            pltpu.SMEM(lengths.shape, jnp.int32),
            pltpu.VMEM(query_grads.shape, bf16),
            pltpu.VMEM((2, 64, 1024), bf16),
            pltpu.VMEM((3, 64, 256), f32),
            pltpu.VMEM((3, 64, 256), f32),
            pltpu.VMEM((EX, 1024), f32),
            pltpu.VMEM((16, EX, 1024), f32),
            pltpu.VMEM((16, 16, 512), bf16),
            pltpu.VMEM((LANES, 1024), f32),
            pltpu.VMEM((2, LANES, LANES), f32),
            dma((4, 2)), dma((4,)), dma((4,)),
            dma((3,)), dma((3,)),
            dma((15,)), dma((16,)),
            dma((15,)), dma((16,)),
        ],
        compiler_params=pltpu.CompilerParams(
            collective_id=0, has_side_effects=True, vmem_limit_bytes=63 * 1024 * 1024
        ),
    )(activations, out_grads, proj_in.T, proj_out.T, lengths, query_grads)


def per_device(small, activations, out_grads, proj_in, proj_out, lengths, query_grads):
    fits = (
        small
        and activations.shape[0] == EX * 4 * LEN
        and proj_in.shape[1] == 32
        and proj_out.shape[1] == 32
        and lengths.shape[0] == EX
        and query_grads.shape == (EX, 1024)
    )
    body = fused if fits else general
    return body(activations, out_grads, proj_in, proj_out, lengths, query_grads)


def solution(mesh):
    small = mesh.shape["dp"] == 4 and mesh.shape["sub"] == 4
    in_specs = (
        P(("groups", "dp"), "sub"),
        P(("groups", "dp"), "sub"),
        P("sub", None),
        P("sub", None),
        P(("groups", "dp", "sub")),
        P(("groups", "dp", "sub"), None),
    )
    out_specs = P(("groups", "dp", "sub"), None)
    return jax.shard_map(
        functools.partial(per_device, small),
        mesh=mesh, in_specs=in_specs, out_specs=out_specs, check_vma=False,
    )
```

```python
import functools

import jax
import jax.numpy as jnp
from jax import lax
from jax.experimental import pallas as pl
from jax.experimental.pallas import tpu as pltpu
from jax.sharding import PartitionSpec as P

LEN = 32
EX = 8
LANES = 128
STEPS = 7
HI = lax.Precision.HIGHEST
MESH = pl.DeviceIdType.MESH
NT = (((1,), (1,)), ((), ()))


def general(activations, out_grads, proj_in, proj_out, lengths, query_grads):
    local_ex = lengths.shape[0]
    width_in = proj_in.shape[1]
    width_out = proj_out.shape[1]
    width = width_in * width_out
    grad_part = jnp.dot(out_grads, proj_out, preferred_element_type=jnp.float32)
    act_part = jnp.dot(activations, proj_in, preferred_element_type=jnp.float32)
    projected = lax.psum_scatter(
        jnp.concatenate([grad_part, act_part], axis=1), "sub", scatter_dimension=0, tiled=True
    )
    positions = jnp.arange(LEN, dtype=jnp.int32)
    token_mask = (positions[None, :] < lengths[:, None]).astype(jnp.float32)
    grad_tok = projected[:, :width_out].reshape(local_ex, LEN, width_out) * token_mask[:, :, None]
    act_tok = projected[:, width_out:].reshape(local_ex, LEN, width_in)
    factors = jnp.einsum("eto,etn->eon", grad_tok, act_tok, precision=HI).reshape(local_ex, width)
    queries = lax.all_gather(query_grads, ("dp", "sub"), axis=0, tiled=True).astype(jnp.float32)
    right = lax.dot_general(factors, queries, NT, precision=HI)
    right = lax.all_gather(right, ("dp", "sub"), axis=0, tiled=True)
    every = lax.all_gather(factors, ("dp", "sub"), axis=0, tiled=True)
    gram = lax.dot_general(every, every, NT, precision=HI)
    mean_diag = jnp.trace(gram) / width
    system = gram / mean_diag + jnp.eye(gram.shape[0], dtype=jnp.float32)
    low = jnp.linalg.cholesky(system)
    middle = lax.linalg.triangular_solve(
        low, right / jnp.sqrt(mean_diag), left_side=True, lower=True, transpose_a=False
    )
    scores = lax.linalg.triangular_solve(low, middle, left_side=True, lower=True, transpose_a=True)
    place = lax.axis_index("dp") * lax.axis_size("sub") + lax.axis_index("sub")
    return lax.dynamic_slice_in_dim(scores, place * local_ex, local_ex, axis=0)


def kernel(
    act_hbm, grad_hbm, pin_hbm, pout_hbm, len_hbm, q_hbm, out_ref,
    act_v, grad_v, pin_v, pout_v, len_v, q_v, spread, part_out, part_in, fac,
    f_all, q_all, q_full, inv_v,
    act_sem, grad_sem, w_sem, ps_sem, pr_sem, fs_sem, fr_sem, qs_sem, qr_sem,
):
    f32, bf16 = jnp.float32, jnp.bfloat16
    dp = lax.axis_index("dp")
    sub = lax.axis_index("sub")
    me = dp * 4 + sub
    core = lax.rem(sub, 2)
    chip = dp * 2 + sub // 2
    mate = sub + 1 - 2 * core
    cross = lax.rem(sub + 2, 4)
    cross_mate = lax.rem(mate + 2, 4)

    to_mate, to_cross = {"sub": mate}, {"sub": cross}
    peers = []
    for dz, dx in ((2, 1), (1, 1), (3, 1), (2, 0), (1, 0), (3, 0), (0, 1)):
        z, u = lax.rem(dp + dz, 4), lax.rem(sub + 2 * dx, 4)
        peers.append((z * 4 + u, {"dp": z, "sub": u}))
    barrier = pltpu.get_barrier_semaphore()
    for where in [w for _, w in peers] + [to_mate]:
        pl.semaphore_signal(barrier, inc=1, device_id=where, device_id_type=MESH)

    w_copies = [
        pltpu.make_async_copy(pout_hbm, pout_v, w_sem.at[0]),
        pltpu.make_async_copy(pin_hbm, pin_v, w_sem.at[1]),
        pltpu.make_async_copy(len_hbm, len_v, w_sem.at[2]),
        pltpu.make_async_copy(q_hbm, q_v, w_sem.at[3]),
    ]
    for c in w_copies:
        c.start()
    order = (cross_mate, cross, mate, sub)
    loads = []
    for i, b in enumerate(order):
        row = pl.multiple_of(b * 256, 256)
        group = [
            pltpu.make_async_copy(
                grad_hbm.at[pl.ds(row, 256)], grad_v.at[i], grad_sem.at[i]
            )
        ]
        for h in range(2):
            group.append(
                pltpu.make_async_copy(
                    act_hbm.at[pl.ds(pl.multiple_of(row + 128 * h, 128), 128)],
                    act_v.at[i, pl.ds(128 * h, 128)],
                    act_sem.at[i, h],
                )
            )
        for c in group:
            c.start()
        loads.append(group)

    row = lax.broadcasted_iota(jnp.int32, (64, 1024), 0)
    col = lax.broadcasted_iota(jnp.int32, (64, 1024), 1)
    spread[0] = jnp.where(row == col // 32, 1.0, 0.0).astype(bf16)
    spread[1] = jnp.where(row == 32 + col % 32, 1.0, 0.0).astype(bf16)
    tok = lax.broadcasted_iota(jnp.int32, (LANES, LANES), 0)
    lane = lax.broadcasted_iota(jnp.int32, (LANES, LANES), 1)
    eye = jnp.where(tok == lane, 1.0, 0.0).astype(f32)

    def push(src, dst, ssem, rsem, where):
        c = pltpu.make_async_remote_copy(
            src_ref=src, dst_ref=dst, send_sem=ssem, recv_sem=rsem,
            device_id=where, device_id_type=MESH,
        )
        c.start()
        return c

    def arrive(dst, ssem, rsem, where):
        pltpu.make_async_remote_copy(
            src_ref=dst, dst_ref=dst, send_sem=ssem, recv_sem=rsem,
            device_id=where, device_id_type=MESH,
        ).wait_recv()

    sent = []
    for c in w_copies:
        c.wait()
    q = q_v[...].astype(f32)
    q_all[me] = jnp.concatenate([q[:, :512], q[:, 512:]], axis=0).astype(bf16)
    token = lax.broadcasted_iota(jnp.int32, (8, 256), 1)
    limit = jnp.zeros((8, 256), jnp.int32)
    for e in range(EX):
        limit = jnp.where(token // LEN == e, len_v[e], limit)
    live = jnp.where(token % LEN < limit, 1.0, 0.0)[:1]

    def project(i):
        for c in loads[i]:
            c.wait()
        g = lax.dot_general(pout_v[...], grad_v[i], NT, preferred_element_type=f32)
        a = lax.dot_general(pin_v[...], act_v[i], NT, preferred_element_type=f32)
        return jnp.concatenate([g, a], axis=0)

    pl.semaphore_wait(barrier, 8)
    hosts = peers + [(me + mate - sub, to_mate)]
    for i, (p, where) in enumerate(hosts):
        sent.append(push(q_all.at[me], q_all.at[me], qs_sem.at[i], qr_sem.at[me], where))
    part_out[0] = project(0)
    sent.append(push(part_out.at[0], part_in.at[0], ps_sem.at[0], pr_sem.at[0], to_mate))
    block = project(1)
    arrive(part_in.at[0], ps_sem.at[0], pr_sem.at[0], to_mate)
    part_out[1] = block + part_in[0]
    sent.append(push(part_out.at[1], part_in.at[1], ps_sem.at[1], pr_sem.at[1], to_cross))
    part_out[2] = project(2)
    sent.append(push(part_out.at[2], part_in.at[2], ps_sem.at[2], pr_sem.at[2], to_mate))
    block = project(3)
    arrive(part_in.at[2], ps_sem.at[2], pr_sem.at[2], to_mate)
    block = block + part_in[2]
    arrive(part_in.at[1], ps_sem.at[1], pr_sem.at[1], to_cross)
    total = ((block + part_in[1]) * live).T

    t1 = total.astype(bf16)
    rest = total - t1.astype(f32)
    t2 = rest.astype(bf16)
    t3 = (rest - t2.astype(f32)).astype(bf16)

    def widen(m):
        return (
            jnp.dot(t1, spread[m], preferred_element_type=f32)
            + jnp.dot(t2, spread[m], preferred_element_type=f32)
            + jnp.dot(t3, spread[m], preferred_element_type=f32)
        )

    prod = widen(0) * widen(1)
    for e in range(EX):
        fac[e:e + 1, :] = jnp.sum(prod[LEN * e:LEN * (e + 1)], axis=0, keepdims=True)
    f_all[me] = fac[...]
    for i, (p, where) in enumerate(hosts):
        sent.append(push(fac, f_all.at[me], fs_sem.at[i], fr_sem.at[me], where))
    for i, (p, where) in enumerate(peers):
        arrive(q_all.at[p], qs_sem.at[i], qr_sem.at[p], where)
        sent.append(push(q_all.at[p], q_all.at[p], qs_sem.at[8 + i], qr_sem.at[p], to_mate))
    for i, (p, where) in enumerate(hosts):
        slot = p + mate - sub if i < 7 else p
        arrive(q_all.at[slot], qs_sem.at[i], qr_sem.at[slot], to_mate)
    for d in range(16):
        q = q_all[d].astype(f32)
        q_full[8 * d:8 * d + 8, :512] = q[:8]
        q_full[8 * d:8 * d + 8, 512:] = q[8:]
    for i in (6, 4, 5, 3, 1, 2, 0):
        p, where = peers[i]
        arrive(f_all.at[p], fs_sem.at[i], fr_sem.at[p], where)
        sent.append(push(f_all.at[p], f_all.at[p], fs_sem.at[8 + i], fr_sem.at[p], to_mate))
    for i, (p, where) in enumerate(hosts):
        slot = p + mate - sub if i < 7 else p
        arrive(f_all.at[slot], fs_sem.at[i], fr_sem.at[slot], to_mate)

    every = f_all[...].reshape(LANES, 1024)
    e1 = every.astype(bf16)
    rest = every - e1.astype(f32)
    e2 = rest.astype(bf16)
    e3 = (rest - e2.astype(f32)).astype(bf16)
    queries = q_full[...].astype(bf16)

    def nt(x, y):
        return lax.dot_general(x, y, NT, preferred_element_type=f32)

    side = nt(e1, e2) + nt(e1, e3)
    gram = nt(e2, e2) + (side + side.T) + nt(e1, e1)
    right = (nt(e3, queries) + nt(e2, queries)) + nt(e1, queries)

    def split(x):
        x1 = x.astype(bf16)
        rest = x - x1.astype(f32)
        x2 = rest.astype(bf16)
        return x1, x2, (rest - x2.astype(f32)).astype(bf16)

    def dot(x, y):
        x1, x2, x3 = split(x)
        y1, y2, y3 = split(y)
        return jnp.dot(
            jnp.concatenate([x2, x3, x1, x2, x1, x1], axis=1),
            jnp.concatenate([y2, y1, y3, y1, y2, y1], axis=0),
            preferred_element_type=f32,
        )

    def whole(x, op):
        return op(op(x, axis=0, keepdims=True), axis=1, keepdims=True)

    mean_diag = whole(gram * eye, jnp.sum) / 1024.0
    scaled = gram / mean_diag
    system = scaled + eye
    frob = jnp.sqrt(whole(scaled * scaled, jnp.sum))
    rowsum = jnp.max(jnp.sum(jnp.abs(scaled), axis=0, keepdims=True), axis=1, keepdims=True)
    top = 1.0 + 1.0001 * jnp.minimum(frob, rowsum)
    r = (top - 1.0) / (top + 1.0)
    start = 2.0 / (1.0 + top)
    res = eye - start * system
    inv = start * eye
    for k in range(STEPS):
        s = 2.0 / (2.0 - r * r)
        if k == 0:
            step = start * res
            square = dot(res, res)
        elif k < STEPS - 1:
            out = dot(jnp.concatenate([inv, res], axis=0), res)
            step, square = out[:LANES], out[LANES:]
        else:
            step = dot(inv, res)
        inv = s * (inv + step)
        if k < STEPS - 1:
            res = s * square + (1.0 - s) * eye
        r = r * r / (2.0 - r * r)
    right = right / jnp.sqrt(mean_diag)
    first = dot(inv, right)
    miss = right - dot(system, first)
    inv_v[0] = inv
    inv_v[1] = first
    mine = pl.ds(pl.multiple_of(me * EX, EX), EX)
    out_ref[...] = inv_v[1, mine, :] + dot(inv_v[0, mine, :], miss)

    for c in sent:
        c.wait_send()


def fused(activations, out_grads, proj_in, proj_out, lengths, query_grads):
    f32, bf16 = jnp.float32, jnp.bfloat16
    d_in, d_out = activations.shape[1], out_grads.shape[1]
    dma = pltpu.SemaphoreType.DMA
    return pl.pallas_call(
        kernel,
        out_shape=pltpu.VMEM((EX, LANES), f32),
        in_specs=[pl.BlockSpec(memory_space=pl.ANY)] * 6,
        out_specs=pl.BlockSpec(memory_space=pltpu.VMEM),
        scratch_shapes=[
            pltpu.VMEM((4, 256, d_in), bf16),
            pltpu.VMEM((4, 256, d_out), bf16),
            pltpu.VMEM(proj_in.shape[::-1], bf16),
            pltpu.VMEM(proj_out.shape[::-1], bf16),
            pltpu.SMEM(lengths.shape, jnp.int32),
            pltpu.VMEM(query_grads.shape, bf16),
            pltpu.VMEM((2, 64, 1024), bf16),
            pltpu.VMEM((3, 64, 256), f32),
            pltpu.VMEM((3, 64, 256), f32),
            pltpu.VMEM((EX, 1024), f32),
            pltpu.VMEM((16, EX, 1024), f32),
            pltpu.VMEM((16, 16, 512), bf16),
            pltpu.VMEM((LANES, 1024), f32),
            pltpu.VMEM((2, LANES, LANES), f32),
            dma((4, 2)), dma((4,)), dma((4,)),
            dma((3,)), dma((3,)),
            dma((15,)), dma((16,)),
            dma((15,)), dma((16,)),
        ],
        compiler_params=pltpu.CompilerParams(
            collective_id=0, has_side_effects=True, vmem_limit_bytes=63 * 1024 * 1024
        ),
    )(activations, out_grads, proj_in.T, proj_out.T, lengths, query_grads)


def per_device(small, activations, out_grads, proj_in, proj_out, lengths, query_grads):
    fits = (
        small
        and activations.shape[0] == EX * 4 * LEN
        and proj_in.shape[1] == 32
        and proj_out.shape[1] == 32
        and lengths.shape[0] == EX
        and query_grads.shape == (EX, 1024)
    )
    body = fused if fits else general
    return body(activations, out_grads, proj_in, proj_out, lengths, query_grads)


def solution(mesh):
    small = mesh.shape["dp"] == 4 and mesh.shape["sub"] == 4
    in_specs = (
        P(("groups", "dp"), "sub"),
        P(("groups", "dp"), "sub"),
        P("sub", None),
        P("sub", None),
        P(("groups", "dp", "sub")),
        P(("groups", "dp", "sub"), None),
    )
    out_specs = P(("groups", "dp", "sub"), None)
    return jax.shard_map(
        functools.partial(per_device, small),
        mesh=mesh, in_specs=in_specs, out_specs=out_specs, check_vma=False,
    )
```
